512 devices in a mesh: sx: 8 (over y), sy: 16 (over x, z_lo, core), blk: 4 (over z_hi).
Axes of the slice: x: 4, y: 8, z: 8 (z_hi: 4, z_lo: 2; z = z_hi * 2 + z_lo), core: 2. Of those that a mesh axis runs over, the one named last changes fastest.
Arguments:
- snapshots: bfloat16 [4, 320, 262144], P('blk', None, ('sx', 'sy')), may hold values from -6 to 6
- offsets: int32 [4], P('blk'), may hold values from 0 to 64
- freqs: int32 [64], replicated, may hold values from 1 to 127, as said below
- modes: bfloat16 [64, 2, 8, 262144], P('blk', None, None, ('sx', 'sy')), may hold values from -6 to 6
- cell_weights: float32 [262144], P(('sx', 'sy')), may hold values from 0.5 to 2
- filter_weights: float32 [64, 8], P('blk'), may hold values from 0.05 to 1
Outputs:
- filtered: bfloat16 [4, 256, 262144], P('blk', None, ('sx', 'sy'))
The draws below stay inside these ranges and needn't reach their ends.
Inputs may be any that keep to these rules, and one draw needn't show every extreme that they name: `freqs`: distinct values; both 1 and 127 appear.
All inputs are finite; a program needn't handle non-finite values.
Results may differ from the reference program's by a relative error of at most 0.018.
Values may be sent and summed in bfloat16 or wider, within the bound.
A program may use at most 64 MiB of HBM per device.

```python
import math
import jax
import jax.numpy as jnp
from jax import lax

NFFT = 256
NF = 64
K = 8
SHIFT = 64
NB = 4
NCELLS = 262144


def draw_freqs(key, part):
    key = jax.random.fold_in(key, 7)
    inner = jax.random.permutation(key, NFFT // 2 - 3) + 2
    chosen = inner[:NF - 2].astype(jnp.int32)
    ends = jnp.array([1, NFFT // 2 - 1], dtype=jnp.int32)
    return jnp.concatenate([ends, chosen]).astype(jnp.int32)


def with_ends(result, rng, least, largest):
    shape = result.shape
    place = [jax.random.randint(jax.random.fold_in(rng, axis), (), 0, shape[axis]) for axis in range(len(shape))]
    result = result.at[tuple(place)].set(least)
    longest = shape.index(max(shape))
    place[longest] = (place[longest] + 1) % shape[longest]
    return result.at[tuple(place)].set(largest)


def block_scale(stream_key, dims, pieces, smallest, high):
    def one(position, shards_of):
        steps = jax.random.uniform(jax.random.fold_in(jax.random.fold_in(stream_key, 6), position), (shards_of,), jnp.float32, smallest / len(pieces), high / len(pieces))
        return jnp.repeat(jnp.exp(steps), dims[position] // shards_of).reshape((-1,) + (1,) * (len(dims) - position - 1))

    factor_of = one(*pieces[0])
    for cut in pieces[1:]:
        factor_of = factor_of * one(*cut)
    return factor_of


def normal_values(stream_key, shape, spread, reach, split=(), held_as=jnp.bfloat16):
    factor_of = block_scale(stream_key, shape, split, -0.22, 0.18) if split else 1.0
    values = jax.random.normal(stream_key, shape, jnp.float32) * spread * factor_of
    return jnp.minimum(jnp.maximum(values, -reach), reach).astype(held_as)


def setup_inputs(seed: int = 0) -> dict:
    seeds = jax.random.split(jax.random.key(seed), 7)
    return {
        "snapshots": normal_values(seeds[0], (NB, NFFT + SHIFT, NCELLS), 1.0, 6.0, ((0, 4), (2, 128))),
        "offsets": with_ends(jax.random.randint(seeds[1], (NB,), 0, SHIFT + 1), jax.random.fold_in(seeds[1], 1), 0, SHIFT).astype(jnp.int32),
        "freqs": draw_freqs(jax.random.fold_in(seeds[6], 71), 0),
        "modes": normal_values(seeds[3], (NF, 2, K, NCELLS), 1.0, 6.0, ((0, 4), (3, 128))),
        "cell_weights": jnp.clip(jnp.exp(math.log(2.0) - 1.3862944 * jax.random.uniform(seeds[4], (NCELLS,), jnp.float32) ** block_scale(seeds[4], (NCELLS,), ((0, 128),), -0.2, 0.2)), 0.5, 2.0),
        "filter_weights": jnp.clip(jnp.exp(math.log(1.0) - 2.9957323 * jax.random.uniform(seeds[5], (NF, K), jnp.float32) ** block_scale(seeds[5], (NF, K), ((0, 4),), -0.2, 0.2)), 0.05, 1.0),
    }


def dft_tables(freqs, length):
    times = jnp.arange(length, dtype=jnp.int32)
    phase = freqs[:, None] * times[None, :] % length
    angle = phase.astype(jnp.float32) * (2.0 * math.pi / length)
    stacked = jnp.stack([jnp.cos(angle), -jnp.sin(angle)], axis=1).reshape(2 * freqs.shape[0], length)
    forward = (stacked / math.sqrt(length)).astype(jnp.bfloat16)
    inverse = (stacked.T / math.sqrt(freqs.shape[0])).astype(jnp.bfloat16)
    return (forward, inverse)

def reference(snapshots, offsets, freqs, modes, cell_weights, filter_weights):
    forward, inverse = dft_tables(freqs, NFFT)
    spectra_list = []
    for block_id in range(NB):
        window = lax.dynamic_slice_in_dim(snapshots[block_id], offsets[block_id].astype(jnp.int32), NFFT, 0)
        spectrum = jnp.dot(forward, window, preferred_element_type=jnp.float32).astype(jnp.bfloat16)
        spectra_list.append(spectrum.reshape(NF, 2, NCELLS))
    spectra = jnp.stack(spectra_list, axis=0)
    weighted = (spectra.astype(jnp.float32) * cell_weights.astype(jnp.float32)).astype(jnp.bfloat16)
    modes_wide = modes.astype(jnp.float32)
    product = jnp.einsum('bfrc,fskc->bfrsk', weighted.astype(jnp.float32), modes_wide, precision=lax.Precision.HIGHEST)
    scale_factor = 1.0 / math.sqrt(NCELLS)
    coeff_real = (product[:, :, 0, 0] + product[:, :, 1, 1]) * scale_factor
    coeff_imag = (product[:, :, 1, 0] - product[:, :, 0, 1]) * scale_factor
    scaled_real = (filter_weights[None] * coeff_real).astype(jnp.bfloat16).astype(jnp.float32)
    scaled_imag = (filter_weights[None] * coeff_imag).astype(jnp.bfloat16).astype(jnp.float32)
    rebuilt_real = jnp.einsum('fkc,bfk->bfc', modes_wide[:, 0], scaled_real, precision=lax.Precision.HIGHEST) - jnp.einsum('fkc,bfk->bfc', modes_wide[:, 1], scaled_imag, precision=lax.Precision.HIGHEST)
    rebuilt_imag = jnp.einsum('fkc,bfk->bfc', modes_wide[:, 0], scaled_imag, precision=lax.Precision.HIGHEST) + jnp.einsum('fkc,bfk->bfc', modes_wide[:, 1], scaled_real, precision=lax.Precision.HIGHEST)
    rebuilt = jnp.stack([rebuilt_real, rebuilt_imag], axis=2).astype(jnp.bfloat16)
    outputs = []
    for block_id in range(NB):
        flat_block = rebuilt[block_id].reshape(2 * NF, NCELLS)
        outputs.append(jnp.dot(inverse, flat_block, preferred_element_type=jnp.float32).astype(jnp.bfloat16))
    return jnp.stack(outputs, axis=0)
```

```python
import functools
import math

import jax
import jax.numpy as jnp
from jax import lax
from jax.experimental import pallas as pl
from jax.experimental.pallas import tpu as pltpu
from jax.sharding import PartitionSpec as P

NFFT = 256
NF = 64
K = 8
NB = 4
Q = 2
GROUP = NF // NB
J = GROUP // Q
RB = 2 * J
RQ = NB * RB
MQ = J * 2 * K
TILE = 512
MESH = pl.DeviceIdType.MESH


def unit_cosine(step):
    folded = jnp.minimum(step, 256 - step)
    x = (64 - folded).astype(jnp.float32) * (math.pi / 128)
    y = x * x
    poly = 1.0 / 362880 - y * (1.0 / 39916800)
    poly = -1.0 / 5040 + y * poly
    poly = 1.0 / 120 + y * poly
    poly = -1.0 / 6 + y * poly
    return x + x * y * poly


def row_frequency(row, me):
    partner = (row // RB) % NB
    return ((me + partner) % NB) * GROUP + (row // RQ) * J + row % J


def row_part(row):
    return (row // J) % 2


def kernel(
    sizes, cells_all, off_ref, freqs_ref, gain_ref, cw_ref, snap_hbm, modes_hbm,
    ret_ref, inv_ref,
    snap, modes, tab, spec, recv, reb, own, first, second,
    load_sem, fsend, frecv, rsend, rrecv, psend, precv, out_sem,
):
    nx, ny = sizes
    me, ix, iy = lax.axis_index("blk"), lax.axis_index("sx"), lax.axis_index("sy")
    cells = snap.shape[1]

    load_snap = pltpu.make_async_copy(snap_hbm.at[0], snap, load_sem.at[0])
    load_modes = pltpu.make_async_copy(modes_hbm, modes, load_sem.at[1])
    load_snap.start()
    load_modes.start()

    barrier = pltpu.get_barrier_semaphore()
    for d in range(1, NB):
        pl.semaphore_signal(barrier, inc=1, device_id={"blk": (me + d) % NB}, device_id_type=MESH)

    @pl.loop(1, ny)
    def _(d):
        pl.semaphore_signal(barrier, inc=1, device_id={"sy": lax.rem(iy + d, ny)}, device_id_type=MESH)

    @pl.loop(1, nx)
    def _(d):
        pl.semaphore_signal(barrier, inc=1, device_id={"sx": lax.rem(ix + d, nx)}, device_id_type=MESH)

    rows, seg = tab.shape
    fr = jnp.broadcast_to(freqs_ref[...].astype(jnp.float32), (rows, NF))
    row = lax.broadcasted_iota(jnp.int32, (rows, NF), 0)
    hit = lax.broadcasted_iota(jnp.int32, (rows, NF), 1) == row_frequency(row, me)
    fcol = jnp.sum(jnp.where(hit, fr, 0.0), axis=1, keepdims=True).astype(jnp.int32)
    part = row_part(lax.broadcasted_iota(jnp.int32, (rows, 1), 0))
    time = lax.broadcasted_iota(jnp.int32, (rows, seg), 1) - off_ref[0]
    value = unit_cosine((fcol * time + 64 * part) & 255) * (1.0 / math.sqrt(NFFT))
    inside = (time >= 0) & (time < NFFT)
    tab[...] = jnp.where(inside, value, 0.0).astype(jnp.bfloat16)

    load_snap.wait()

    def forward_copy(q, d):
        return pltpu.make_async_remote_copy(
            src_ref=spec.at[pl.ds(q * RQ + d * RB, RB)],
            dst_ref=recv.at[pl.ds(q * RQ + d * RB, RB)],
            send_sem=fsend.at[q, d], recv_sem=frecv.at[q, d],
            device_id={"blk": (me + d) % NB}, device_id_type=MESH,
        )

    def back_copy(q, d):
        return pltpu.make_async_remote_copy(
            src_ref=reb.at[pl.ds(q * RQ + d * RB, RB)],
            dst_ref=ret_ref.at[pl.ds(q * RQ + d * RB, RB)],
            send_sem=rsend.at[q, d], recv_sem=rrecv.at[q, d],
            device_id={"blk": (me + NB - d) % NB}, device_id_type=MESH,
        )

    for q in range(Q):
        rows_q = pl.ds(q * RQ, RQ)
        for c in range(0, cells, TILE):
            s = jnp.dot(
                tab[rows_q, :], snap[:, pl.ds(c, TILE)], preferred_element_type=jnp.float32
            ).astype(jnp.bfloat16)
            spec[rows_q, pl.ds(c, TILE)] = s
        if q == 0:
            pl.semaphore_wait(barrier, NB - 1 + ny - 1 + nx - 1)
        for d in (2, 1, 3):
            forward_copy(q, d).start()

    sel_row = lax.broadcasted_iota(jnp.int32, (NF, rows), 1)
    sel = lax.broadcasted_iota(jnp.int32, (NF, rows), 0) == row_frequency(sel_row, me)
    fb = jnp.broadcast_to(freqs_ref[...], (8, NF)).astype(jnp.float32).astype(jnp.bfloat16)
    flane = jnp.dot(
        fb, sel.astype(jnp.float32).astype(jnp.bfloat16), preferred_element_type=jnp.float32
    )[0:1].astype(jnp.int32)
    part = row_part(lax.broadcasted_iota(jnp.int32, (1, rows), 1))
    time = lax.broadcasted_iota(jnp.int32, (NFFT, rows), 0)
    inv_ref[...] = (
        unit_cosine((flane * time + 64 * part) & 255) * (1.0 / math.sqrt(NF))
    ).astype(jnp.bfloat16)

    lane = lax.broadcasted_iota(jnp.int32, (K, Q * MQ), 1)
    spread = (lane % K == lax.broadcasted_iota(jnp.int32, (K, Q * MQ), 0)).astype(jnp.float32)
    wide = jnp.dot(
        gain_ref[...], spread, precision=lax.Precision.HIGHEST, preferred_element_type=jnp.float32
    )
    lane = lax.broadcasted_iota(jnp.int32, (GROUP, Q * MQ), 1)
    mine = lane // (2 * K) == lax.broadcasted_iota(jnp.int32, (GROUP, Q * MQ), 0)
    gains = jnp.sum(jnp.where(mine, wide, 0.0), axis=0, keepdims=True)
    lane = lax.broadcasted_iota(jnp.int32, (J, MQ), 1)
    diagonal = lane // (2 * K) == lax.broadcasted_iota(jnp.int32, (J, MQ), 0)
    lane8 = lax.broadcasted_iota(jnp.int32, (2 * NB, MQ), 1)
    side = (lane8 // K) % 2
    turn = lax.broadcasted_iota(jnp.int32, (2 * NB, MQ), 0) % 2
    scale = 1.0 / math.sqrt(cells_all)

    load_modes.wait()

    def exchange(q, stage, axis, n, index, buffer):
        @pl.loop(1, n)
        def _(d):
            pltpu.make_async_remote_copy(
                src_ref=own.at[q, stage], dst_ref=buffer.at[q, d - 1],
                send_sem=psend.at[q, stage], recv_sem=precv.at[q, stage],
                device_id={axis: lax.rem(index + d, n)}, device_id_type=MESH,
            ).start()

        pltpu.make_async_copy(buffer.at[q], buffer.at[q], precv.at[q, stage]).wait()
        return own[q, stage] + jnp.sum(buffer[q], axis=0)

    for q in range(Q):
        rows_q = pl.ds(q * RQ, RQ)
        modes_q = pl.ds(q * MQ, MQ)
        for d in range(1, NB):
            forward_copy(q, d).wait_recv()
        product = jnp.zeros((RQ, MQ), jnp.float32)
        for c in range(0, cells, TILE):
            cols = pl.ds(c, TILE)
            local = spec[pl.ds(q * RQ, RB), cols]
            others = recv[pl.ds(q * RQ + RB, RQ - RB), cols]
            x = jnp.concatenate([local, others], axis=0)
            weighted = (x.astype(jnp.float32) * cw_ref[:, cols]).astype(jnp.bfloat16)
            product += lax.dot_general(
                weighted, modes[modes_q, cols], (((1,), (1,)), ((), ())),
                preferred_element_type=jnp.float32,
            )
        product = product.reshape(2 * NB, J, MQ)
        coeff = jnp.sum(jnp.where(diagonal[None], product, 0.0), axis=1)
        own[q, 0] = coeff
        own[q, 1] = exchange(q, 0, "sy", ny, iy, first)
        total = exchange(q, 1, "sx", nx, ix, second)
        crossed = jnp.where(side == 0, pltpu.roll(total, MQ - K, 1), pltpu.roll(total, K, 1))
        crossed = jnp.where(turn == 0, pltpu.roll(crossed, 2 * NB - 1, 0), pltpu.roll(crossed, 1, 0))
        both = jnp.where(side == turn, total + crossed, total - crossed)
        scaled = gains[:, q * MQ : (q + 1) * MQ] * (both * scale)
        table = jnp.where(diagonal[None], scaled[:, None, :], 0.0).reshape(RQ, MQ)
        table = table.astype(jnp.bfloat16)
        for c in range(0, cells, TILE):
            cols = pl.ds(c, TILE)
            reb[rows_q, cols] = jnp.dot(
                table, modes[modes_q, cols], preferred_element_type=jnp.float32
            ).astype(jnp.bfloat16)
        for d in (2, 1, 3):
            back_copy(q, d).start()
        pltpu.make_async_copy(
            reb.at[pl.ds(q * RQ, RB)], ret_ref.at[pl.ds(q * RQ, RB)], out_sem.at[q]
        ).start()

    for q in range(Q):
        for d in range(1, NB):
            forward_copy(q, d).wait_send()
            back_copy(q, d).wait()
        pltpu.make_async_copy(
            reb.at[pl.ds(q * RQ, RB)], ret_ref.at[pl.ds(q * RQ, RB)], out_sem.at[q]
        ).wait()
        for stage, buffer in ((0, first), (1, second)):
            pltpu.make_async_copy(buffer.at[q], buffer.at[q], psend.at[q, stage]).wait()


def inverse_kernel(inv_ref, ret_ref, out_ref):
    out_ref[0] = jnp.dot(
        inv_ref[...], ret_ref[...], preferred_element_type=jnp.float32
    ).astype(jnp.bfloat16)


def solution(mesh):
    nx, ny = mesh.shape["sx"], mesh.shape["sy"]

    def per_device(snapshots, offsets, freqs, modes, cell_weights, filter_weights):
        seg, cells = snapshots.shape[1:]
        vmem = pl.BlockSpec(memory_space=pltpu.VMEM)
        anywhere = pl.BlockSpec(memory_space=pl.ANY)
        bf16 = jnp.bfloat16
        returned, inverse = pl.pallas_call(
            functools.partial(kernel, (nx, ny), cells * nx * ny),
            out_shape=(
                jax.ShapeDtypeStruct((2 * NF, cells), bf16),
                jax.ShapeDtypeStruct((NFFT, 2 * NF), bf16),
            ),
            in_specs=[
                pl.BlockSpec(memory_space=pltpu.SMEM), vmem, vmem, vmem, anywhere, anywhere,
            ],
            out_specs=(anywhere, vmem),
            scratch_shapes=[
                pltpu.VMEM((seg, cells), bf16),
                pltpu.VMEM((GROUP * 2 * K, cells), bf16),
                pltpu.VMEM((2 * NF, seg), bf16),
                pltpu.VMEM((2 * NF, cells), bf16),
                pltpu.VMEM((2 * NF, cells), bf16),
                pltpu.VMEM((2 * NF, cells), bf16),
                pltpu.VMEM((Q, 2, 2 * NB, MQ), jnp.float32),
                pltpu.VMEM((Q, ny - 1, 2 * NB, MQ), jnp.float32),
                pltpu.VMEM((Q, nx - 1, 2 * NB, MQ), jnp.float32),
                pltpu.SemaphoreType.DMA((2,)),
                pltpu.SemaphoreType.DMA((Q, NB)),
                pltpu.SemaphoreType.DMA((Q, NB)),
                pltpu.SemaphoreType.DMA((Q, NB)),
                pltpu.SemaphoreType.DMA((Q, NB)),
                pltpu.SemaphoreType.DMA((Q, 2)),
                pltpu.SemaphoreType.DMA((Q, 2)),
                pltpu.SemaphoreType.DMA((Q,)),
            ],
            compiler_params=pltpu.CompilerParams(
                collective_id=0, has_side_effects=True, vmem_limit_bytes=48 * 2**20
            ),
            name="exchange",
        )(
            offsets, freqs.reshape(1, NF), filter_weights, cell_weights.reshape(1, cells),
            snapshots, modes.reshape(GROUP * 2 * K, cells),
        )
        tile = min(1024, cells)
        return pl.pallas_call(
            inverse_kernel,
            grid=(cells // tile,),
            out_shape=jax.ShapeDtypeStruct((1, NFFT, cells), bf16),
            in_specs=[
                pl.BlockSpec((NFFT, 2 * NF), lambda i: (0, 0)),
                pl.BlockSpec((2 * NF, tile), lambda i: (0, i)),
            ],
            out_specs=pl.BlockSpec((1, NFFT, tile), lambda i: (0, 0, i)),
            name="inverse",
        )(inverse, returned)

    placed = (
        P("blk", None, ("sx", "sy")),
        P("blk"),
        P(),
        P("blk", None, None, ("sx", "sy")),
        P(("sx", "sy")),
        P("blk", None),
    )
    return jax.shard_map(
        per_device, mesh=mesh, in_specs=placed,
        out_specs=P("blk", None, ("sx", "sy")), check_vma=False,
    )
```

```python
import functools
import math

import jax
import jax.numpy as jnp
from jax import lax
from jax.experimental import pallas as pl
from jax.experimental.pallas import tpu as pltpu
from jax.sharding import PartitionSpec as P

NFFT = 256
NF = 64
K = 8
NB = 4
Q = 4
GROUP = NF // NB
J = GROUP // Q
E = 2 * J
H = 2
RB = H * E
RQ = NB * RB
TQ = NB * E
LANES = 128
TILE = 512
MESH = pl.DeviceIdType.MESH


def unit_cosine(step):
    folded = jnp.minimum(step, 256 - step)
    x = (64 - folded).astype(jnp.float32) * (math.pi / 128)
    y = x * x
    poly = 1.0 / 362880 - y * (1.0 / 39916800)
    poly = -1.0 / 5040 + y * poly
    poly = 1.0 / 120 + y * poly
    poly = -1.0 / 6 + y * poly
    return x + x * y * poly


def row_frequency(row, me):
    partner = (row // E) % NB
    return ((me + partner) % NB) * GROUP + (row // TQ) * J + row % J


def row_part(row):
    return (row // J) % 2


def halves_together(parts):
    return jnp.concatenate(
        [parts[h][d * E : (d + 1) * E] for d in range(NB) for h in range(H)], axis=0
    )


def sum_of_four(x, j):
    x = x + jnp.where(j == J - 1, pltpu.roll(x, J - 1, 0), pltpu.roll(x, E - 1, 0))
    return x + jnp.where(j >= 2, pltpu.roll(x, 2, 0), pltpu.roll(x, E - 2, 0))


def kernel(
    sizes, cells_all, off_ref, freqs_hbm, gain_hbm, cw_hbm, snap_hbm, modes_hbm,
    ret_ref, inv_ref,
    freqs_ref, gain_ref, cw_ref, snap, modes,
    tab, spec, recv, reb, own, first, second,
    load_sem, fsend, frecv, rsend, rrecv, psend, precv, out_sem,
):
    nx, ny = sizes
    me, ix, iy = lax.axis_index("blk"), lax.axis_index("sx"), lax.axis_index("sy")
    half = spec.shape[1]

    loads = [
        pltpu.make_async_copy(src, dst, load_sem.at[i])
        for i, (src, dst) in enumerate(
            (
                (freqs_hbm, freqs_ref), (snap_hbm.at[0], snap),
                (gain_hbm, gain_ref), (cw_hbm, cw_ref), (modes_hbm, modes),
            )
        )
    ]
    for load in loads:
        load.start()

    barrier = pltpu.get_barrier_semaphore()
    for d in range(1, NB):
        pl.semaphore_signal(barrier, inc=1, device_id={"blk": (me + d) % NB}, device_id_type=MESH)

    @pl.loop(1, nx)
    def _(d):
        pl.semaphore_signal(barrier, inc=1, device_id={"sx": lax.rem(ix + d, nx)}, device_id_type=MESH)

    @pl.loop(1, ny)
    def _(d):
        pl.semaphore_signal(barrier, inc=1, device_id={"sy": lax.rem(iy + d, ny)}, device_id_type=MESH)

    loads[0].wait()
    rows, seg = tab.shape
    fr = jnp.broadcast_to(freqs_ref[...].astype(jnp.float32), (rows, NF))
    row = lax.broadcasted_iota(jnp.int32, (rows, NF), 0)
    hit = lax.broadcasted_iota(jnp.int32, (rows, NF), 1) == row_frequency(row, me)
    fcol = jnp.sum(jnp.where(hit, fr, 0.0), axis=1, keepdims=True).astype(jnp.int32)
    part = row_part(lax.broadcasted_iota(jnp.int32, (rows, 1), 0))
    time = lax.broadcasted_iota(jnp.int32, (rows, seg), 1) - off_ref[0]
    value = unit_cosine((fcol * time + 64 * part) & 255) * (1.0 / math.sqrt(NFFT))
    inside = (time >= 0) & (time < NFFT)
    tab[...] = jnp.where(inside, value, 0.0).astype(jnp.bfloat16)

    def forward_copy(q, d):
        return pltpu.make_async_remote_copy(
            src_ref=spec.at[pl.ds(q * RQ + d * RB, RB)],
            dst_ref=recv.at[pl.ds(q * RQ + d * RB, RB)],
            send_sem=fsend.at[q, d], recv_sem=frecv.at[q, d],
            device_id={"blk": (me + d) % NB}, device_id_type=MESH,
        )

    def back_copy(q, d):
        return pltpu.make_async_remote_copy(
            src_ref=reb.at[pl.ds(q * RQ + d * RB, RB)],
            dst_ref=ret_ref.at[pl.ds(q * RQ + d * RB, RB)],
            send_sem=rsend.at[q, d], recv_sem=rrecv.at[q, d],
            device_id={"blk": (me + NB - d) % NB}, device_id_type=MESH,
        )

    def transform(q):
        for c in range(0, half, TILE):
            parts = [
                jnp.dot(
                    tab[pl.ds(q * TQ, TQ), :], snap[:, pl.ds(h * half + c, TILE)],
                    preferred_element_type=jnp.float32,
                )
                for h in range(H)
            ]
            spec[pl.ds(q * RQ, RQ), pl.ds(c, TILE)] = halves_together(parts).astype(jnp.bfloat16)

    def send_forward(q):
        for d in (2, 1, 3):
            if q:
                forward_copy(q - 1, d).wait_send()
            forward_copy(q, d).start()

    loads[1].wait()
    transform(0)
    pl.semaphore_wait(barrier, NB - 1 + ny - 1 + nx - 1)
    send_forward(0)
    for q in range(1, Q):
        transform(q)

    sel_row = lax.broadcasted_iota(jnp.int32, (NF, rows), 1)
    sel = lax.broadcasted_iota(jnp.int32, (NF, rows), 0) == row_frequency(sel_row, me)
    fb = jnp.broadcast_to(freqs_ref[...], (8, NF)).astype(jnp.float32).astype(jnp.bfloat16)
    flane = jnp.dot(
        fb, sel.astype(jnp.float32).astype(jnp.bfloat16), preferred_element_type=jnp.float32
    )[0:1].astype(jnp.int32)
    part = row_part(lax.broadcasted_iota(jnp.int32, (1, rows), 1))
    time = lax.broadcasted_iota(jnp.int32, (NFFT, rows), 0)
    inv_ref[...] = (
        unit_cosine((flane * time + 64 * part) & 255) * (1.0 / math.sqrt(NF))
    ).astype(jnp.bfloat16)

    send_forward(1)

    loads[2].wait()
    all_lanes = GROUP * 2 * K
    lane = lax.broadcasted_iota(jnp.int32, (K, all_lanes), 1)
    spread = (lane % K == lax.broadcasted_iota(jnp.int32, (K, all_lanes), 0)).astype(jnp.float32)
    wide = lax.dot_general(
        gain_ref[...], spread, (((0,), (0,)), ((), ())),
        precision=lax.Precision.HIGHEST, preferred_element_type=jnp.float32,
    )
    lane = lax.broadcasted_iota(jnp.int32, (GROUP, all_lanes), 1)
    mine = lane // (2 * K) == lax.broadcasted_iota(jnp.int32, (GROUP, all_lanes), 0)
    gains = jnp.sum(jnp.where(mine, wide, 0.0), axis=0, keepdims=True)

    row = lax.broadcasted_iota(jnp.int32, (E, LANES), 0)
    lane = lax.broadcasted_iota(jnp.int32, (E, LANES), 1)
    j, turn, side = row % J, row // J, (lane // K) % 2
    scale = 1.0 / math.sqrt(cells_all)

    def diagonal(q):
        return lane // (2 * K) == (q % 2) * J + j

    loads[3].wait()
    loads[4].wait()

    def spread_out(q, stage, axis, n, index, buffer):
        @pl.loop(1, n)
        def _(d):
            pltpu.make_async_remote_copy(
                src_ref=own.at[q, stage], dst_ref=buffer.at[q, d - 1],
                send_sem=psend.at[q, stage], recv_sem=precv.at[q, stage],
                device_id={axis: lax.rem(index + d, n)}, device_id_type=MESH,
            ).start()

    def total_of(q, stage, buffer):
        pltpu.make_async_copy(buffer.at[q], buffer.at[q], precv.at[q, stage]).wait()
        return own[q, stage] + jnp.sum(buffer[q], axis=0)

    def project(q):
        for d in range(1, NB):
            forward_copy(q, d).wait_recv()
        modes_q = pl.ds(q // 2 * LANES, LANES)
        product = jnp.zeros((TQ, LANES), jnp.float32)
        for c in range(0, half, TILE):
            cols = pl.ds(c, TILE)
            x = jnp.concatenate(
                [spec[pl.ds(q * RQ, RB), cols], recv[pl.ds(q * RQ + RB, RQ - RB), cols]], axis=0
            ).astype(jnp.float32)
            for h in range(H):
                cells = pl.ds(h * half + c, TILE)
                xh = jnp.concatenate(
                    [x[(d * H + h) * E : (d * H + h + 1) * E] for d in range(NB)], axis=0
                )
                product += lax.dot_general(
                    (xh * cw_ref[:, cells]).astype(jnp.bfloat16), modes[modes_q, cells],
                    (((1,), (1,)), ((), ())), preferred_element_type=jnp.float32,
                )
        coeff = jnp.zeros((E, LANES), jnp.float32)
        for d in range(NB):
            sums = sum_of_four(jnp.where(diagonal(q), product[d * E : (d + 1) * E], 0.0), j)
            coeff += jnp.where(j == d, sums, 0.0)
        own[q, 0] = coeff
        spread_out(q, 0, "sy", ny, iy, first)

    def pass_on(q):
        own[q, 1] = total_of(q, 0, first)
        spread_out(q, 1, "sx", nx, ix, second)

    def rebuild(q):
        total = total_of(q, 1, second)
        crossed = jnp.where(
            side == 0, pltpu.roll(total, LANES - K, 1), pltpu.roll(total, K, 1)
        )
        crossed = pltpu.roll(crossed, J, 0)
        both = jnp.where(side == turn, total + crossed, total - crossed)
        scaled = gains[:, q // 2 * LANES : (q // 2 + 1) * LANES] * (both * scale)
        table = jnp.concatenate(
            [
                jnp.where(diagonal(q), sum_of_four(jnp.where(j == d, scaled, 0.0), j), 0.0)
                for d in range(NB)
            ],
            axis=0,
        ).astype(jnp.bfloat16)
        modes_q = pl.ds(q // 2 * LANES, LANES)
        for c in range(0, half, TILE):
            parts = [
                jnp.dot(
                    table, modes[modes_q, pl.ds(h * half + c, TILE)],
                    preferred_element_type=jnp.float32,
                )
                for h in range(H)
            ]
            reb[pl.ds(q * RQ, RQ), pl.ds(c, TILE)] = halves_together(parts).astype(jnp.bfloat16)
        for d in (2, 1, 3):
            back_copy(q, d).start()
        keep(q).start()

    def keep(q):
        return pltpu.make_async_copy(
            reb.at[pl.ds(q * RQ, RB)], ret_ref.at[pl.ds(q * RQ, RB)], out_sem.at[q]
        )

    send_forward(2)
    send_forward(3)
    project(0)
    project(1)
    pass_on(0)
    project(2)
    pass_on(1)
    project(3)
    rebuild(0)
    pass_on(2)
    rebuild(1)
    pass_on(3)
    rebuild(2)
    rebuild(3)

    for d in range(1, NB):
        forward_copy(Q - 1, d).wait_send()
    for q in range(Q):
        for stage, buffer in ((0, first), (1, second)):
            pltpu.make_async_copy(buffer.at[q], buffer.at[q], psend.at[q, stage]).wait()
        for d in range(1, NB):
            back_copy(q, d).wait()
        keep(q).wait()


def inverse_kernel(inv_ref, ret_ref, out_ref):
    tile = out_ref.shape[2]
    per_half = ret_ref.shape[1] // tile
    step = pl.program_id(0)
    cols = pl.ds(pl.multiple_of(lax.rem(step, per_half) * tile, tile), tile)
    x = ret_ref[:, cols].astype(jnp.float32).reshape(Q * NB, H, E, tile)
    x = jnp.where(step < per_half, x[:, 0], x[:, 1]).reshape(2 * NF, tile)
    out_ref[0] = jnp.dot(
        inv_ref[...], x.astype(jnp.bfloat16), preferred_element_type=jnp.float32
    ).astype(jnp.bfloat16)


def solution(mesh):
    nx, ny = mesh.shape["sx"], mesh.shape["sy"]

    def per_device(snapshots, offsets, freqs, modes, cell_weights, filter_weights):
        seg, cells = snapshots.shape[1:]
        half = cells // H
        vmem = pl.BlockSpec(memory_space=pltpu.VMEM)
        hbm = pl.BlockSpec(memory_space=pltpu.HBM)
        bf16, f32, dma = jnp.bfloat16, jnp.float32, pltpu.SemaphoreType.DMA
        returned, inverse = pl.pallas_call(
            functools.partial(kernel, (nx, ny), cells * nx * ny),
            out_shape=(
                jax.ShapeDtypeStruct((Q * RQ, half), bf16),
                jax.ShapeDtypeStruct((NFFT, 2 * NF), bf16),
            ),
            in_specs=[pl.BlockSpec(memory_space=pltpu.SMEM)] + [hbm] * 5,
            out_specs=(vmem, vmem),
            scratch_shapes=[
                pltpu.VMEM((1, NF), jnp.int32),
                pltpu.VMEM((K, GROUP), f32),
                pltpu.VMEM((1, cells), f32),
                pltpu.VMEM((seg, cells), bf16),
                pltpu.VMEM((GROUP * 2 * K, cells), bf16),
                pltpu.VMEM((2 * NF, seg), bf16),
                pltpu.VMEM((Q * RQ, half), bf16),
                pltpu.VMEM((Q * RQ, half), bf16),
                pltpu.VMEM((Q * RQ, half), bf16),
                pltpu.VMEM((Q, 2, E, LANES), f32),
                pltpu.VMEM((Q, ny - 1, E, LANES), f32),
                pltpu.VMEM((Q, nx - 1, E, LANES), f32),
                dma((5,)), dma((Q, NB)), dma((Q, NB)), dma((Q, NB)), dma((Q, NB)),
                dma((Q, 2)), dma((Q, 2)), dma((Q,)),
            ],
            compiler_params=pltpu.CompilerParams(
                collective_id=0, has_side_effects=True, vmem_limit_bytes=32 * 2**20
            ),
            name="exchange",
        )(
            offsets,
            *(
                pltpu.with_memory_space_constraint(x, pltpu.HBM)
                for x in (
                    freqs.reshape(1, NF), filter_weights.T, cell_weights.reshape(1, cells),
                    snapshots, modes.reshape(GROUP * 2 * K, cells),
                )
            ),
        )
        tile = min(TILE, half)
        return pl.pallas_call(
            inverse_kernel,
            grid=(cells // tile,),
            out_shape=jax.ShapeDtypeStruct((1, NFFT, cells), bf16),
            in_specs=[vmem, vmem],
            out_specs=pl.BlockSpec((1, NFFT, tile), lambda i: (0, 0, i)),
            compiler_params=pltpu.CompilerParams(vmem_limit_bytes=16 * 2**20),
            name="inverse",
        )(inverse, returned)

    placed = (
        P("blk", None, ("sx", "sy")),
        P("blk"),
        P(),
        P("blk", None, None, ("sx", "sy")),
        P(("sx", "sy")),
        P("blk", None),
    )
    return jax.shard_map(
        per_device, mesh=mesh, in_specs=placed,
        out_specs=P("blk", None, ("sx", "sy")), check_vma=False,
    )
```

```python
import functools
import math

import jax
import jax.numpy as jnp
from jax import lax
from jax.experimental import pallas as pl
from jax.experimental.pallas import tpu as pltpu
from jax.sharding import PartitionSpec as P

NFFT = 256
NF = 64
K = 8
NB = 4
Q = 4
GROUP = NF // NB
J = GROUP // Q
E = 2 * J
H = 2
RB = H * E
RQ = NB * RB
TQ = NB * E
LANES = 128
TILE = 512
INNER = 4
MESH = pl.DeviceIdType.MESH


def unit_cosine(step):
    folded = jnp.minimum(step, 256 - step)
    x = (64 - folded).astype(jnp.float32) * (math.pi / 128)
    y = x * x
    poly = 1.0 / 362880 - y * (1.0 / 39916800)
    poly = -1.0 / 5040 + y * poly
    poly = 1.0 / 120 + y * poly
    poly = -1.0 / 6 + y * poly
    return x + x * y * poly


def row_frequency(row, me):
    partner = (row // E) % NB
    return ((me + partner) % NB) * GROUP + (row // TQ) * J + row % J


def row_part(row):
    return (row // J) % 2


def halves_together(parts):
    return jnp.concatenate(
        [parts[h][d * E : (d + 1) * E] for d in range(NB) for h in range(H)], axis=0
    )


def sum_of_four(x, j):
    x = x + jnp.where(j == J - 1, pltpu.roll(x, J - 1, 0), pltpu.roll(x, E - 1, 0))
    return x + jnp.where(j >= 2, pltpu.roll(x, 2, 0), pltpu.roll(x, E - 2, 0))


def kernel(
    sizes, cells_all, off_ref, freqs_hbm, gain_hbm, cw_hbm, snap_hbm, modes_hbm,
    ret_ref, inv_ref,
    freqs_ref, gain_ref, cw_ref, snap, modes,
    tab, spec, recv, reb, own, first, second,
    load_sem, fsend, frecv, rsend, rrecv, psend, precv, out_sem,
):
    nx, ny = sizes
    me, ix, iy = lax.axis_index("blk"), lax.axis_index("sx"), lax.axis_index("sy")
    half = spec.shape[1]

    loads = [
        pltpu.make_async_copy(src, dst, load_sem.at[i])
        for i, (src, dst) in enumerate(
            (
                (freqs_hbm, freqs_ref), (snap_hbm.at[0], snap),
                (gain_hbm, gain_ref), (cw_hbm, cw_ref), (modes_hbm, modes),
            )
        )
    ]
    for load in loads:
        load.start()

    barrier = pltpu.get_barrier_semaphore()
    for d in range(1, NB):
        pl.semaphore_signal(barrier, inc=1, device_id={"blk": (me + d) % NB}, device_id_type=MESH)

    stages = (
        (first, ny, lambda d: {"sy": (iy + d) % ny}),
        (second, nx, lambda d: {"sx": (ix + d) % nx}),
    )
    greeted = NB - 1
    for _, n, partner in stages:
        greeted += n - 1
        for d in range(1, n):
            pl.semaphore_signal(barrier, inc=1, device_id=partner(d), device_id_type=MESH)

    loads[0].wait()
    rows = tab.shape[0]

    def make_table(start, count):
        fr = jnp.broadcast_to(freqs_ref[...].astype(jnp.float32), (count, NF))
        row = lax.broadcasted_iota(jnp.int32, (count, NF), 0) + start
        hit = lax.broadcasted_iota(jnp.int32, (count, NF), 1) == row_frequency(row, me)
        fcol = jnp.sum(jnp.where(hit, fr, 0.0), axis=1, keepdims=True).astype(jnp.int32)
        part = row_part(lax.broadcasted_iota(jnp.int32, (count, 1), 0) + start)
        time = lax.broadcasted_iota(jnp.int32, (count, NFFT), 1) - off_ref[0]
        value = unit_cosine((fcol * time + 64 * part) & 255) * (1.0 / math.sqrt(NFFT))
        tab[pl.ds(start, count)] = value.astype(jnp.bfloat16)

    make_table(0, TQ)

    def forward_copy(q, d):
        return pltpu.make_async_remote_copy(
            src_ref=spec.at[pl.ds(q * RQ + d * RB, RB)],
            dst_ref=recv.at[pl.ds(q * RQ + d * RB, RB)],
            send_sem=fsend.at[q, d], recv_sem=frecv.at[q, d],
            device_id={"blk": (me + d) % NB}, device_id_type=MESH,
        )

    def back_copy(q, d):
        return pltpu.make_async_remote_copy(
            src_ref=reb.at[pl.ds(q * RQ + d * RB, RB)],
            dst_ref=ret_ref.at[pl.ds(q * RQ + d * RB, RB)],
            send_sem=rsend.at[q, d], recv_sem=rrecv.at[q, d],
            device_id={"blk": (me + NB - d) % NB}, device_id_type=MESH,
        )

    def transform(q):
        for c in range(0, half, TILE):
            parts = [
                jnp.dot(
                    tab[pl.ds(q * TQ, TQ), :], snap[pl.ds(0, NFFT), pl.ds(h * half + c, TILE)],
                    preferred_element_type=jnp.float32,
                )
                for h in range(H)
            ]
            spec[pl.ds(q * RQ, RQ), pl.ds(c, TILE)] = halves_together(parts).astype(jnp.bfloat16)

    def send_forward(q):
        for d in (2, 1, 3):
            if q:
                forward_copy(q - 1, d).wait_send()
            forward_copy(q, d).start()

    loads[1].wait()
    extra = snap.shape[0] - NFFT
    early = lax.broadcasted_iota(jnp.int32, (extra, TILE), 0) < off_ref[0]
    for c in range(0, snap.shape[1], TILE):
        cols = pl.ds(c, TILE)
        low, high = snap[pl.ds(0, extra), cols], snap[pl.ds(NFFT, extra), cols]
        snap[pl.ds(0, extra), cols] = jnp.where(early, high, low)
    transform(0)
    pl.semaphore_wait(barrier, greeted)
    send_forward(0)
    make_table(TQ, rows - TQ)
    for q in range(1, Q):
        transform(q)

    sel_row = lax.broadcasted_iota(jnp.int32, (NF, rows), 1)
    sel = lax.broadcasted_iota(jnp.int32, (NF, rows), 0) == row_frequency(sel_row, me)
    fb = jnp.broadcast_to(freqs_ref[...], (8, NF)).astype(jnp.float32).astype(jnp.bfloat16)
    flane = jnp.dot(
        fb, sel.astype(jnp.float32).astype(jnp.bfloat16), preferred_element_type=jnp.float32
    )[0:1].astype(jnp.int32)
    part = row_part(lax.broadcasted_iota(jnp.int32, (1, rows), 1))
    time = lax.broadcasted_iota(jnp.int32, (NFFT, rows), 0)
    inv_ref[...] = (
        unit_cosine((flane * time + 64 * part) & 255) * (1.0 / math.sqrt(NF))
    ).astype(jnp.bfloat16)

    send_forward(1)

    loads[2].wait()
    all_lanes = GROUP * 2 * K
    lane = lax.broadcasted_iota(jnp.int32, (K, all_lanes), 1)
    spread = (lane % K == lax.broadcasted_iota(jnp.int32, (K, all_lanes), 0)).astype(jnp.float32)
    wide = lax.dot_general(
        gain_ref[...], spread, (((0,), (0,)), ((), ())),
        precision=lax.Precision.HIGHEST, preferred_element_type=jnp.float32,
    )
    lane = lax.broadcasted_iota(jnp.int32, (GROUP, all_lanes), 1)
    mine = lane // (2 * K) == lax.broadcasted_iota(jnp.int32, (GROUP, all_lanes), 0)
    gains = jnp.sum(jnp.where(mine, wide, 0.0), axis=0, keepdims=True)

    row = lax.broadcasted_iota(jnp.int32, (E, LANES), 0)
    lane = lax.broadcasted_iota(jnp.int32, (E, LANES), 1)
    j, turn, side = row % J, row // J, (lane // K) % 2
    scale = 1.0 / math.sqrt(cells_all)

    def diagonal(q):
        return lane // (2 * K) == (q % 2) * J + j

    loads[3].wait()
    loads[4].wait()

    def spread_out(q, stage):
        buffer, n, partner = stages[stage]
        for d in sorted(range(1, n), key=lambda d: abs(d - n // 2)):
            pltpu.make_async_remote_copy(
                src_ref=own.at[q, stage], dst_ref=buffer.at[q, d - 1],
                send_sem=psend.at[q, stage], recv_sem=precv.at[q, stage],
                device_id=partner(d), device_id_type=MESH,
            ).start()

    def total_of(q, stage):
        buffer, n, _ = stages[stage]
        total = own[q, stage]
        if n > 1:
            pltpu.make_async_copy(buffer.at[q], buffer.at[q], precv.at[q, stage]).wait()
            total += jnp.sum(buffer[q], axis=0)
        return total

    def project(q):
        for d in range(1, NB):
            forward_copy(q, d).wait_recv()
        modes_q = pl.ds(q // 2 * LANES, LANES)
        product = jnp.zeros((TQ, LANES), jnp.float32)
        for c in range(0, half, TILE):
            cols = pl.ds(c, TILE)
            x = jnp.concatenate(
                [spec[pl.ds(q * RQ, RB), cols], recv[pl.ds(q * RQ + RB, RQ - RB), cols]], axis=0
            ).astype(jnp.float32)
            for h in range(H):
                cells = pl.ds(h * half + c, TILE)
                xh = jnp.concatenate(
                    [x[(d * H + h) * E : (d * H + h + 1) * E] for d in range(NB)], axis=0
                )
                product += lax.dot_general(
                    (xh * cw_ref[:, cells]).astype(jnp.bfloat16), modes[modes_q, cells],
                    (((1,), (1,)), ((), ())), preferred_element_type=jnp.float32,
                )
        coeff = jnp.zeros((E, LANES), jnp.float32)
        for d in range(NB):
            sums = sum_of_four(jnp.where(diagonal(q), product[d * E : (d + 1) * E], 0.0), j)
            coeff += jnp.where(j == d, sums, 0.0)
        own[q, 0] = coeff
        spread_out(q, 0)

    def pass_on(q, stage):
        own[q, stage] = total_of(q, stage - 1)
        spread_out(q, stage)

    def rebuild(q):
        total = total_of(q, 1)
        crossed = jnp.where(
            side == 0, pltpu.roll(total, LANES - K, 1), pltpu.roll(total, K, 1)
        )
        crossed = pltpu.roll(crossed, J, 0)
        both = jnp.where(side == turn, total + crossed, total - crossed)
        scaled = gains[:, q // 2 * LANES : (q // 2 + 1) * LANES] * (both * scale)
        table = jnp.concatenate(
            [
                jnp.where(diagonal(q), sum_of_four(jnp.where(j == d, scaled, 0.0), j), 0.0)
                for d in range(NB)
            ],
            axis=0,
        ).astype(jnp.bfloat16)
        modes_q = pl.ds(q // 2 * LANES, LANES)
        for c in range(0, half, TILE):
            parts = [
                jnp.dot(
                    table, modes[modes_q, pl.ds(h * half + c, TILE)],
                    preferred_element_type=jnp.float32,
                )
                for h in range(H)
            ]
            reb[pl.ds(q * RQ, RQ), pl.ds(c, TILE)] = halves_together(parts).astype(jnp.bfloat16)
        for b in range(NB):

            @pl.when(b != me)
            def _():
                back_copy(q, (me + NB - b) % NB).start()

        keep(q).start()

    def keep(q):
        return pltpu.make_async_copy(
            reb.at[pl.ds(q * RQ, RB)], ret_ref.at[pl.ds(q * RQ, RB)], out_sem.at[q]
        )

    project(0)
    send_forward(2)
    project(1)
    send_forward(3)
    pass_on(0, 1)
    project(2)
    pass_on(1, 1)
    project(3)
    rebuild(0)
    pass_on(2, 1)
    rebuild(1)
    pass_on(3, 1)
    rebuild(2)
    rebuild(3)

    for d in range(1, NB):
        forward_copy(Q - 1, d).wait_send()
    for q in range(Q):
        for stage, (buffer, n, _) in enumerate(stages):
            if n > 1:
                pltpu.make_async_copy(buffer.at[q], buffer.at[q], psend.at[q, stage]).wait()
        for d in range(1, NB):
            back_copy(q, d).wait()
        keep(q).wait()


def inverse_kernel(inv_ref, ret_ref, out_hbm, out, sems):
    half = ret_ref.shape[1]
    copies = []
    for c in range(0, half, TILE):
        x = ret_ref[:, pl.ds(c, TILE)].astype(jnp.float32).reshape(Q * NB, H, E, TILE)
        for h in range(H):
            cols = pl.ds(h * half + c, TILE)
            xh = x[:, h].reshape(2 * NF, TILE).astype(jnp.bfloat16)
            out[:, cols] = jnp.dot(
                inv_ref[...], xh, preferred_element_type=jnp.float32
            ).astype(jnp.bfloat16)
            copy = pltpu.make_async_copy(
                out.at[:, cols], out_hbm.at[0, :, cols], sems.at[len(copies)]
            )
            copy.start()
            copies.append(copy)
    for copy in copies:
        copy.wait()


def solution(mesh):
    nx, ny = mesh.shape["sx"], mesh.shape["sy"]

    def per_device(snapshots, offsets, freqs, modes, cell_weights, filter_weights):
        seg, cells = snapshots.shape[1:]
        half = cells // H
        vmem = pl.BlockSpec(memory_space=pltpu.VMEM)
        hbm = pl.BlockSpec(memory_space=pltpu.HBM)
        bf16, f32, dma = jnp.bfloat16, jnp.float32, pltpu.SemaphoreType.DMA
        returned, inverse = pl.pallas_call(
            functools.partial(kernel, (nx, ny), cells * nx * ny),
            out_shape=(
                jax.ShapeDtypeStruct((Q * RQ, half), bf16),
                jax.ShapeDtypeStruct((NFFT, 2 * NF), bf16),
            ),
            in_specs=[pl.BlockSpec(memory_space=pltpu.SMEM)] + [hbm] * 5,
            out_specs=(vmem, vmem),
            scratch_shapes=[
                pltpu.VMEM((1, NF), jnp.int32),
                pltpu.VMEM((K, GROUP), f32),
                pltpu.VMEM((1, cells), f32),
                pltpu.VMEM((seg, cells), bf16),
                pltpu.VMEM((GROUP * 2 * K, cells), bf16),
                pltpu.VMEM((2 * NF, NFFT), bf16),
                pltpu.VMEM((Q * RQ, half), bf16),
                pltpu.VMEM((Q * RQ, half), bf16),
                pltpu.VMEM((Q * RQ, half), bf16),
                pltpu.VMEM((Q, 3, E, LANES), f32),
                pltpu.VMEM((Q, max(ny - 1, 1), E, LANES), f32),
                pltpu.VMEM((Q, max(nx - 1, 1), E, LANES), f32),
                dma((5,)), dma((Q, NB)), dma((Q, NB)), dma((Q, NB)), dma((Q, NB)),
                dma((Q, 3)), dma((Q, 3)), dma((Q,)),
            ],
            compiler_params=pltpu.CompilerParams(
                collective_id=0, has_side_effects=True, vmem_limit_bytes=32 * 2**20
            ),
            name="exchange",
        )(
            offsets,
            *(
                pltpu.with_memory_space_constraint(x, pltpu.HBM)
                for x in (
                    freqs.reshape(1, NF), filter_weights.T, cell_weights.reshape(1, cells),
                    snapshots, modes.reshape(GROUP * 2 * K, cells),
                )
            ),
        )
        return pl.pallas_call(
            inverse_kernel,
            out_shape=jax.ShapeDtypeStruct((1, NFFT, cells), bf16),
            in_specs=[vmem, vmem],
            out_specs=pl.BlockSpec(memory_space=pl.ANY),
            scratch_shapes=[pltpu.VMEM((NFFT, cells), bf16), dma((cells // TILE,))],
            compiler_params=pltpu.CompilerParams(vmem_limit_bytes=16 * 2**20),
            name="inverse",
        )(inverse, returned)

    placed = (
        P("blk", None, ("sx", "sy")),
        P("blk"),
        P(),
        P("blk", None, None, ("sx", "sy")),
        P(("sx", "sy")),
        P("blk", None),
    )
    return jax.shard_map(
        per_device, mesh=mesh, in_specs=placed,
        out_specs=P("blk", None, ("sx", "sy")), check_vma=False,
    )
```

```python
import functools
import math

import jax
import jax.numpy as jnp
from jax import lax
from jax.experimental import pallas as pl
from jax.experimental.pallas import tpu as pltpu
from jax.sharding import PartitionSpec as P

NFFT = 256
NF = 64
K = 8
NB = 4
Q = 4
GROUP = NF // NB
J = GROUP // Q
E = 2 * J
H = 2
RB = H * E
RQ = NB * RB
TQ = NB * E
LANES = 128
TILE = 512
INNER = 4
MESH = pl.DeviceIdType.MESH


def unit_cosine(step):
    folded = jnp.minimum(step, 256 - step)
    x = (64 - folded).astype(jnp.float32) * (math.pi / 128)
    y = x * x
    poly = 1.0 / 362880 - y * (1.0 / 39916800)
    poly = -1.0 / 5040 + y * poly
    poly = 1.0 / 120 + y * poly
    poly = -1.0 / 6 + y * poly
    return x + x * y * poly


def row_frequency(row, me):
    partner = (row // E) % NB
    return ((me + partner) % NB) * GROUP + (row // TQ) * J + row % J


def row_part(row):
    return (row // J) % 2


def halves_together(parts):
    return jnp.concatenate(
        [parts[h][d * E : (d + 1) * E] for d in range(NB) for h in range(H)], axis=0
    )


def sum_of_four(x, j):
    x = x + jnp.where(j == J - 1, pltpu.roll(x, J - 1, 0), pltpu.roll(x, E - 1, 0))
    return x + jnp.where(j >= 2, pltpu.roll(x, 2, 0), pltpu.roll(x, E - 2, 0))


def kernel(
    sizes, cells_all, off_ref, freqs_hbm, gain_hbm, cw_hbm, snap_hbm, modes_hbm,
    ret_ref, inv_ref,
    freqs_ref, gain_ref, cw_ref, snap, modes,
    tab, spec, recv, reb, own, first, second,
    load_sem, fsend, frecv, rsend, rrecv, psend, precv, out_sem,
):
    nx, ny = sizes
    me, ix, iy = lax.axis_index("blk"), lax.axis_index("sx"), lax.axis_index("sy")
    half = spec.shape[1]

    stages = (
        (first, ny, lambda d: {"sy": (iy + d) % ny}),
        (second, nx, lambda d: {"sx": (ix + d) % nx}),
    )
    far_first = [
        sorted(range(1, n), key=lambda d: abs(d - n // 2)) for _, n, _ in stages
    ]
    barrier = pltpu.get_barrier_semaphore()
    greeted = [{"blk": (me + 2) % NB}] + [stages[1][2](d) for d in far_first[1]]
    greeted += [{"blk": (me + 1) % NB}, {"blk": (me + 3) % NB}]
    greeted += [stages[0][2](d) for d in far_first[0]]
    for partner in greeted:
        pl.semaphore_signal(barrier, inc=1, device_id=partner, device_id_type=MESH)

    loads = [
        pltpu.make_async_copy(src, dst, load_sem.at[i])
        for i, (src, dst) in enumerate(
            (
                (freqs_hbm, freqs_ref), (snap_hbm.at[0], snap),
                (gain_hbm, gain_ref), (cw_hbm, cw_ref), (modes_hbm, modes),
            )
        )
    ]
    for load in loads:
        load.start()

    loads[0].wait()
    rows = tab.shape[0]

    def make_table(start, count):
        fr = jnp.broadcast_to(freqs_ref[...].astype(jnp.float32), (count, NF))
        row = lax.broadcasted_iota(jnp.int32, (count, NF), 0) + start
        hit = lax.broadcasted_iota(jnp.int32, (count, NF), 1) == row_frequency(row, me)
        fcol = jnp.sum(jnp.where(hit, fr, 0.0), axis=1, keepdims=True).astype(jnp.int32)
        part = row_part(lax.broadcasted_iota(jnp.int32, (count, 1), 0) + start)
        time = lax.broadcasted_iota(jnp.int32, (count, NFFT), 1) - off_ref[0]
        value = unit_cosine((fcol * time + 64 * part) & 255) * (1.0 / math.sqrt(NFFT))
        tab[pl.ds(start, count)] = value.astype(jnp.bfloat16)

    make_table(0, TQ)

    def forward_copy(q, d):
        return pltpu.make_async_remote_copy(
            src_ref=spec.at[pl.ds(q * RQ + d * RB, RB)],
            dst_ref=recv.at[pl.ds(q * RQ + d * RB, RB)],
            send_sem=fsend.at[q, d], recv_sem=frecv.at[q, d],
            device_id={"blk": (me + d) % NB}, device_id_type=MESH,
        )

    def back_copy(q, d):
        return pltpu.make_async_remote_copy(
            src_ref=reb.at[pl.ds(q * RQ + d * RB, RB)],
            dst_ref=ret_ref.at[pl.ds(q * RQ + d * RB, RB)],
            send_sem=rsend.at[q, d], recv_sem=rrecv.at[q, d],
            device_id={"blk": (me + NB - d) % NB}, device_id_type=MESH,
        )

    def transform(q):
        for c in range(0, half, TILE):
            parts = [
                jnp.dot(
                    tab[pl.ds(q * TQ, TQ), :], snap[pl.ds(0, NFFT), pl.ds(h * half + c, TILE)],
                    preferred_element_type=jnp.float32,
                )
                for h in range(H)
            ]
            spec[pl.ds(q * RQ, RQ), pl.ds(c, TILE)] = halves_together(parts).astype(jnp.bfloat16)

    def send_forward(q, partners=(2, 1, 3)):
        for d in partners:
            if q:
                forward_copy(q - 1, d).wait_send()
            forward_copy(q, d).start()

    loads[1].wait()
    extra = snap.shape[0] - NFFT
    early = lax.broadcasted_iota(jnp.int32, (extra, TILE), 0) < off_ref[0]
    for c in range(0, snap.shape[1], TILE):
        cols = pl.ds(c, TILE)
        low, high = snap[pl.ds(0, extra), cols], snap[pl.ds(NFFT, extra), cols]
        snap[pl.ds(0, extra), cols] = jnp.where(early, high, low)
    transform(0)
    pl.semaphore_wait(barrier, len(greeted))
    send_forward(0)
    make_table(TQ, rows - TQ)
    for q in range(1, Q):
        transform(q)

    sel_row = lax.broadcasted_iota(jnp.int32, (NF, rows), 1)
    sel = lax.broadcasted_iota(jnp.int32, (NF, rows), 0) == row_frequency(sel_row, me)
    fb = jnp.broadcast_to(freqs_ref[...], (8, NF)).astype(jnp.float32).astype(jnp.bfloat16)
    flane = jnp.dot(
        fb, sel.astype(jnp.float32).astype(jnp.bfloat16), preferred_element_type=jnp.float32
    )[0:1].astype(jnp.int32)
    part = row_part(lax.broadcasted_iota(jnp.int32, (1, rows), 1))
    time = lax.broadcasted_iota(jnp.int32, (NFFT, rows), 0)
    inv_ref[...] = (
        unit_cosine((flane * time + 64 * part) & 255) * (1.0 / math.sqrt(NF))
    ).astype(jnp.bfloat16)

    send_forward(1)

    loads[2].wait()
    all_lanes = GROUP * 2 * K
    lane = lax.broadcasted_iota(jnp.int32, (K, all_lanes), 1)
    spread = (lane % K == lax.broadcasted_iota(jnp.int32, (K, all_lanes), 0)).astype(jnp.float32)
    wide = lax.dot_general(
        gain_ref[...], spread, (((0,), (0,)), ((), ())),
        precision=lax.Precision.HIGHEST, preferred_element_type=jnp.float32,
    )
    lane = lax.broadcasted_iota(jnp.int32, (GROUP, all_lanes), 1)
    mine = lane // (2 * K) == lax.broadcasted_iota(jnp.int32, (GROUP, all_lanes), 0)
    gains = jnp.sum(jnp.where(mine, wide, 0.0), axis=0, keepdims=True)

    row = lax.broadcasted_iota(jnp.int32, (E, LANES), 0)
    lane = lax.broadcasted_iota(jnp.int32, (E, LANES), 1)
    j, turn, side = row % J, row // J, (lane // K) % 2
    scale = 1.0 / math.sqrt(cells_all)

    def diagonal(q):
        return lane // (2 * K) == (q % 2) * J + j

    loads[3].wait()
    loads[4].wait()

    def spread_out(q, stage):
        buffer, n, partner = stages[stage]
        for d in far_first[stage]:
            pltpu.make_async_remote_copy(
                src_ref=own.at[q, stage], dst_ref=buffer.at[q, d - 1],
                send_sem=psend.at[q, stage], recv_sem=precv.at[q, stage],
                device_id=partner(d), device_id_type=MESH,
            ).start()

    def total_of(q, stage):
        buffer, n, _ = stages[stage]
        total = own[q, stage]
        if n > 1:
            pltpu.make_async_copy(buffer.at[q], buffer.at[q], precv.at[q, stage]).wait()
            total += jnp.sum(buffer[q], axis=0)
        return total

    slots = (0, K, LANES // 2, LANES // 2 + K)

    def packed(coeff, q):
        crossed = pltpu.roll(pltpu.roll(coeff, LANES - K, 1), J, 0)
        combined = jnp.where(turn == 0, coeff + crossed, coeff - crossed)
        mine = (side == 0) & (lane // (LANES // 2) == q % 2)
        combined = jnp.where(mine, combined, 0.0)
        message = combined
        for i in range(1, NB):
            message += pltpu.roll(pltpu.roll(combined, slots[i], 1), E - 2 * i, 0)
        return message[:2]

    def unpacked(total):
        message = jnp.concatenate([total] * NB, axis=0)
        combined = message
        for i in range(1, NB):
            combined = jnp.where(row // 2 == i, pltpu.roll(message, LANES - slots[i], 1), combined)
        crossed = pltpu.roll(pltpu.roll(combined, K, 1), J, 0)
        return jnp.where(side == 0, combined, jnp.where(turn == 0, -crossed, crossed))

    def project(q):
        for d in range(1, NB):
            forward_copy(q, d).wait_recv()
        modes_q = pl.ds(q // 2 * LANES, LANES)
        product = jnp.zeros((TQ, LANES), jnp.float32)
        for c in range(0, half, TILE):
            cols = pl.ds(c, TILE)
            x = jnp.concatenate(
                [spec[pl.ds(q * RQ, RB), cols], recv[pl.ds(q * RQ + RB, RQ - RB), cols]], axis=0
            ).astype(jnp.float32)
            for h in range(H):
                cells = pl.ds(h * half + c, TILE)
                xh = jnp.concatenate(
                    [x[(d * H + h) * E : (d * H + h + 1) * E] for d in range(NB)], axis=0
                )
                product += lax.dot_general(
                    (xh * cw_ref[:, cells]).astype(jnp.bfloat16), modes[modes_q, cells],
                    (((1,), (1,)), ((), ())), preferred_element_type=jnp.float32,
                )
        coeff = jnp.zeros((E, LANES), jnp.float32)
        for d in range(NB):
            sums = sum_of_four(jnp.where(diagonal(q), product[d * E : (d + 1) * E], 0.0), j)
            coeff += jnp.where(j == d, sums, 0.0)
        own[q, 0] = packed(coeff, q)
        spread_out(q, 0)

    def pass_on(q, stage):
        own[q, stage] = total_of(q, stage - 1)
        spread_out(q, stage)

    def rebuild(q):
        both = unpacked(total_of(q, 1))
        scaled = gains[:, q // 2 * LANES : (q // 2 + 1) * LANES] * (both * scale)
        table = jnp.concatenate(
            [
                jnp.where(diagonal(q), sum_of_four(jnp.where(j == d, scaled, 0.0), j), 0.0)
                for d in range(NB)
            ],
            axis=0,
        ).astype(jnp.bfloat16)
        modes_q = pl.ds(q // 2 * LANES, LANES)
        for c in range(0, half, TILE):
            parts = [
                jnp.dot(
                    table, modes[modes_q, pl.ds(h * half + c, TILE)],
                    preferred_element_type=jnp.float32,
                )
                for h in range(H)
            ]
            reb[pl.ds(q * RQ, RQ), pl.ds(c, TILE)] = halves_together(parts).astype(jnp.bfloat16)
        for b in range(NB):

            @pl.when(b != me)
            def _():
                back_copy(q, (me + NB - b) % NB).start()

        keep(q).start()

    def keep(q):
        return pltpu.make_async_copy(
            reb.at[pl.ds(q * RQ, RB)], ret_ref.at[pl.ds(q * RQ, RB)], out_sem.at[q]
        )

    project(0)
    send_forward(2)
    send_forward(3, (2,))
    project(1)
    send_forward(3, (1, 3))
    pass_on(0, 1)
    project(2)
    pass_on(1, 1)
    project(3)
    rebuild(0)
    pass_on(2, 1)
    rebuild(1)
    pass_on(3, 1)
    rebuild(2)
    rebuild(3)

    for d in range(1, NB):
        forward_copy(Q - 1, d).wait_send()
    for q in range(Q):
        for stage, (buffer, n, _) in enumerate(stages):
            if n > 1:
                pltpu.make_async_copy(buffer.at[q], buffer.at[q], psend.at[q, stage]).wait()
        for d in range(1, NB):
            back_copy(q, d).wait()
        keep(q).wait()


def inverse_kernel(inv_ref, ret_ref, out_hbm, out, sems):
    half = ret_ref.shape[1]
    copies = []
    for c in range(0, half, TILE):
        x = ret_ref[:, pl.ds(c, TILE)].astype(jnp.float32).reshape(Q * NB, H, E, TILE)
        for h in range(H):
            cols = pl.ds(h * half + c, TILE)
            xh = x[:, h].reshape(2 * NF, TILE).astype(jnp.bfloat16)
            out[:, cols] = jnp.dot(
                inv_ref[...], xh, preferred_element_type=jnp.float32
            ).astype(jnp.bfloat16)
            copy = pltpu.make_async_copy(
                out.at[:, cols], out_hbm.at[0, :, cols], sems.at[len(copies)]
            )
            copy.start()
            copies.append(copy)
    for copy in copies:
        copy.wait()


def solution(mesh):
    nx, ny = mesh.shape["sx"], mesh.shape["sy"]

    def per_device(snapshots, offsets, freqs, modes, cell_weights, filter_weights):
        seg, cells = snapshots.shape[1:]
        half = cells // H
        vmem = pl.BlockSpec(memory_space=pltpu.VMEM)
        hbm = pl.BlockSpec(memory_space=pltpu.HBM)
        bf16, f32, dma = jnp.bfloat16, jnp.float32, pltpu.SemaphoreType.DMA
        returned, inverse = pl.pallas_call(
            functools.partial(kernel, (nx, ny), cells * nx * ny),
            out_shape=(
                jax.ShapeDtypeStruct((Q * RQ, half), bf16),
                jax.ShapeDtypeStruct((NFFT, 2 * NF), bf16),
            ),
            in_specs=[pl.BlockSpec(memory_space=pltpu.SMEM)] + [hbm] * 5,
            out_specs=(vmem, vmem),
            scratch_shapes=[
                pltpu.VMEM((1, NF), jnp.int32),
                pltpu.VMEM((K, GROUP), f32),
                pltpu.VMEM((1, cells), f32),
                pltpu.VMEM((seg, cells), bf16),
                pltpu.VMEM((GROUP * 2 * K, cells), bf16),
                pltpu.VMEM((2 * NF, NFFT), bf16),
                pltpu.VMEM((Q * RQ, half), bf16),
                pltpu.VMEM((Q * RQ, half), bf16),
                pltpu.VMEM((Q * RQ, half), bf16),
                pltpu.VMEM((Q, 2, 2, LANES), f32),
                pltpu.VMEM((Q, max(ny - 1, 1), 2, LANES), f32),
                pltpu.VMEM((Q, max(nx - 1, 1), 2, LANES), f32),
                dma((5,)), dma((Q, NB)), dma((Q, NB)), dma((Q, NB)), dma((Q, NB)),
                dma((Q, 3)), dma((Q, 3)), dma((Q,)),
            ],
            compiler_params=pltpu.CompilerParams(
                collective_id=0, has_side_effects=True, vmem_limit_bytes=32 * 2**20
            ),
            name="exchange",
        )(
            offsets,
            *(
                pltpu.with_memory_space_constraint(x, pltpu.HBM)
                for x in (
                    freqs.reshape(1, NF), filter_weights.T, cell_weights.reshape(1, cells),
                    snapshots, modes.reshape(GROUP * 2 * K, cells),
                )
            ),
        )
        return pl.pallas_call(
            inverse_kernel,
            out_shape=jax.ShapeDtypeStruct((1, NFFT, cells), bf16),
            in_specs=[vmem, vmem],
            out_specs=pl.BlockSpec(memory_space=pl.ANY),
            scratch_shapes=[pltpu.VMEM((NFFT, cells), bf16), dma((cells // TILE,))],
            compiler_params=pltpu.CompilerParams(vmem_limit_bytes=16 * 2**20),
            name="inverse",
        )(inverse, returned)

    placed = (
        P("blk", None, ("sx", "sy")),
        P("blk"),
        P(),
        P("blk", None, None, ("sx", "sy")),
        P(("sx", "sy")),
        P("blk", None),
    )
    return jax.shard_map(
        per_device, mesh=mesh, in_specs=placed,
        out_specs=P("blk", None, ("sx", "sy")), check_vma=False,
    )
```
